256 devices in a mesh: prow: 16 (over z, core), pcol: 16 (over x, y).
Axes of the slice: x: 4, y: 4, z: 8, core: 2. Of those that a mesh axis runs over, the one named last changes fastest.
Arguments:
- x_done: float32 [2, 512, 32768], P(None, None, 'prow'), may hold values from -6 to 6
- l_below: float32 [2, 2, 1024, 32768], P(None, None, 'pcol', 'prow'), may hold values from -0.0234375 to 0.0234375
- rhs_window: float32 [2, 512, 2, 1024], P(None, 'prow', None, 'pcol'), may hold values from -6 to 6
- inv_diag: float32 [2, 2, 1024, 1024], P(None, None, 'pcol'), may hold values from -0.5 to 2
- l_couple: float32 [2, 1024, 1024], P(None, 'pcol'), may hold values from -0.125 to 0.125
Outputs:
- x_window: float32 [2, 512, 2, 1024], P(None, 'prow', None, 'pcol')
The draws below stay inside these ranges and needn't reach their ends.
All inputs are finite; a program needn't handle non-finite values.
Results may differ from the reference program's by a relative error of at most 0.00007.
Values sent between devices are 32-bit elements; how exact they have to be, the bound alone decides.
No kernel may reach another device: no remote copies, remote signals or barrier semaphores. Data moves between devices by JAX's collectives and lax.ppermute only.
A program may use at most 64 MiB of HBM per device.

```python
import jax
import jax.numpy as jnp
from jax import lax

NB = 1024
ROWS = 32768
RHS = 512


def draw_inv_diag(key, part):
    key = jax.random.fold_in(key, 7)
    factor = NB ** (-0.5)
    random_part = jax.random.truncated_normal(key, -4.0, 4.0, (2, 2, NB, NB), jnp.float32) * factor
    row_ids = lax.broadcasted_iota(jnp.int32, (2, 2, NB, NB), 2)
    col_ids = lax.broadcasted_iota(jnp.int32, (2, 2, NB, NB), 3)
    comp_ids = lax.broadcasted_iota(jnp.int32, (2, 2, NB, NB), 0)
    diagonal = jnp.where((row_ids == col_ids) & (comp_ids == 0), 1.5, 0.0).astype(jnp.float32)
    return random_part + diagonal


def strengthened(drawn, own_key, source, target, parts, factor):
    owner, partner = [(jnp.arange(drawn.shape[axis_at]) // (drawn.shape[axis_at] // parts)).reshape([-1 if axis == axis_at else 1 for axis in range(drawn.ndim)]) for axis_at in (source, target)]
    chosen = jax.random.permutation(own_key, parts)[partner]
    strong = (owner == chosen) | (owner == (partner + parts // 2) % parts)
    return jnp.where(strong, factor * drawn, drawn)


def block_levels(own_key, shape, pieces, least, high):
    gain = 1.0
    for axis_at, parts in pieces:
        draws = jax.random.uniform(jax.random.fold_in(jax.random.fold_in(own_key, 6), axis_at), (parts,), jnp.float32, least / len(pieces), high / len(pieces))
        gain = gain * jnp.repeat(jnp.exp(draws), shape[axis_at] // parts).reshape((-1,) + (1,) * (len(shape) - 1 - axis_at))
    return gain


def bell_draw(rng, shape, deviation, reach, shards=(), dtype=jnp.bfloat16):
    gain = block_levels(rng, shape, shards, -0.22, 0.18) if shards else 1.0
    array = jax.random.normal(rng, shape, jnp.float32) * deviation * gain
    return jnp.minimum(jnp.maximum(array, -reach), reach).astype(dtype)


def gaussian_with(key, dims, width, limit, cuts, heavy, kind=jnp.bfloat16):
    array = width * jax.random.normal(key, dims, jnp.float32)
    if cuts:
        array = array * block_levels(key, dims, cuts, -0.22, 0.18)
    return jnp.clip(strengthened(array, jax.random.fold_in(key, 3), *heavy), -limit, limit).astype(kind)


def setup_inputs(seed: int = 0) -> dict:
    key_of = jax.random.split(jax.random.key(seed), 6)
    return {
        "x_done": gaussian_with(key_of[0], (2, RHS, ROWS), 1.0, 6.0, ((2, 16),), (2, 1, 16, 2.0), jnp.float32),
        "l_below": bell_draw(key_of[1], (2, 2, NB, ROWS), (2 * ROWS) ** -0.5, 0.0234375, ((2, 16), (3, 16)), jnp.float32),
        "rhs_window": bell_draw(key_of[2], (2, RHS, 2, NB), 1.0, 6.0, ((1, 16), (3, 16)), jnp.float32),
        "inv_diag": draw_inv_diag(jax.random.fold_in(key_of[5], 71), 0),
        "l_couple": bell_draw(key_of[4], (2, NB, NB), (2 * NB) ** -0.5, 0.125, ((1, 16),), jnp.float32),
    }


highest = lax.Precision.HIGHEST


def dot_last(left_mat, right_mat):
    return lax.dot_general(left_mat, right_mat, (((left_mat.ndim - 1,), (1,)), ((), ())), precision=highest, preferred_element_type=jnp.float32)


def conj_apply(left_re, left_im, right_re, right_im):
    real_out = dot_last(left_re, right_re) + dot_last(left_im, right_im)
    imag_out = dot_last(left_im, right_re) - dot_last(left_re, right_im)
    return real_out, imag_out


def plain_apply(left_re, left_im, right_re, right_im):
    real_out = dot_last(left_re, right_re) - dot_last(left_im, right_im)
    imag_out = dot_last(left_re, right_im) + dot_last(left_im, right_re)
    return real_out, imag_out


def reference(x_done, l_below, rhs_window, inv_diag, l_couple):
    row_ids = lax.broadcasted_iota(jnp.int32, (NB, NB), 0)
    col_ids = lax.broadcasted_iota(jnp.int32, (NB, NB), 1)
    upper_mask = (col_ids >= row_ids).astype(jnp.float32)
    inv_masked = inv_diag * upper_mask
    joined = l_below.reshape(2, 2 * NB, ROWS)
    update_re, update_im = conj_apply(x_done[0], x_done[1], joined[0], joined[1])
    update = jnp.stack([update_re, update_im]).reshape(2, RHS, 2, NB)
    reduced = rhs_window - update
    one_re, one_im = plain_apply(reduced[0, :, 1], reduced[1, :, 1], inv_masked[0, 1], inv_masked[1, 1])
    coupling_re, coupling_im = conj_apply(one_re, one_im, l_couple[0], l_couple[1])
    zero_in_re = reduced[0, :, 0] - coupling_re
    zero_in_im = reduced[1, :, 0] - coupling_im
    zero_re, zero_im = plain_apply(zero_in_re, zero_in_im, inv_masked[0, 0], inv_masked[1, 0])
    real_part = jnp.stack([zero_re, one_re], axis=1)
    imag_part = jnp.stack([zero_im, one_im], axis=1)
    return jnp.stack([real_part, imag_part])
```

```python
import jax
import jax.numpy as jnp
from jax import lax
from jax.experimental import pallas as pl
from jax.experimental.pallas import tpu as pltpu
from jax.sharding import PartitionSpec as P

BF = jnp.bfloat16
F32 = jnp.float32
K_STEPS = 8
VMEM_LIMIT = 48 * 1024 * 1024


def split(mat):
    high = mat.astype(BF)
    return high, (mat - high.astype(F32)).astype(BF)


def dot_split(left, right):
    left_high, left_low = split(left)
    right_high, right_low = split(right)
    return lax.dot_general(
        jnp.concatenate([left_high, left_low, left_high], axis=1),
        jnp.concatenate([right_high, right_high, right_low], axis=1),
        (((1,), (1,)), ((), ())),
        preferred_element_type=F32,
    )


def update_kernel(core_ref, x_ref, l_ref, rhs_ref, keep_ref, send_ref, packed_ref, total):
    step = pl.program_id(0)
    left = jnp.concatenate([x_ref[0], x_ref[1]], axis=1)
    rows = []
    for panel in range(2):
        real, imag = l_ref[0, panel], l_ref[1, panel]
        rows.append(jnp.concatenate([real, imag], axis=1))
        rows.append(jnp.concatenate([-imag, real], axis=1))
    term = dot_split(left, jnp.concatenate(rows, axis=0))

    @pl.when(step == 0)
    def _():
        total[...] = term
        packed_ref[...] = jnp.concatenate(
            [rhs_ref[part, :, panel, :] for panel in range(2) for part in range(2)], axis=1
        )

    @pl.when(step > 0)
    def _():
        total[...] += term

    @pl.when(step == K_STEPS - 1)
    def _():
        core = core_ref[0]
        blocks, rows_each = keep_ref.shape[0], keep_ref.shape[1]
        for block in range(blocks):
            base = 2 * rows_each * block
            keep_ref[block] = total[pl.ds(pl.multiple_of(base + core * rows_each, 8), rows_each), :]
            send_ref[block] = total[pl.ds(pl.multiple_of(base + (1 - core) * rows_each, 8), rows_each), :]


def update(core, x_done, l_below, rhs_window):
    _, sides, depth = x_done.shape
    width = l_below.shape[2]
    rows = rhs_window.shape[1]
    blocks = sides // (2 * rows)
    chunk = depth // K_STEPS
    half = jax.ShapeDtypeStruct((blocks, rows, 4 * width), F32)
    whole = lambda step: (0, 0, 0)
    return pl.pallas_call(
        update_kernel,
        grid=(K_STEPS,),
        in_specs=[
            pl.BlockSpec(memory_space=pltpu.SMEM),
            pl.BlockSpec((2, sides, chunk), lambda step: (0, 0, step)),
            pl.BlockSpec((2, 2, width, chunk), lambda step: (0, 0, 0, step)),
            pl.BlockSpec(rhs_window.shape, lambda step: (0, 0, 0, 0)),
        ],
        out_specs=[
            pl.BlockSpec(half.shape, whole),
            pl.BlockSpec(half.shape, whole),
            pl.BlockSpec((rows, 4 * width), lambda step: (0, 0)),
        ],
        out_shape=[half, half, jax.ShapeDtypeStruct((rows, 4 * width), F32)],
        scratch_shapes=[pltpu.VMEM((sides, 4 * width), F32)],
        compiler_params=pltpu.CompilerParams(vmem_limit_bytes=VMEM_LIMIT),
        cost_estimate=pl.CostEstimate(
            flops=2 * 3 * sides * 2 * depth * 4 * width, bytes_accessed=x_done.size * 4 + l_below.size * 4, transcendentals=0
        ),
    )(core, x_done, l_below, rhs_window)


def reduce_kernel(parts_ref, packed_ref, zero_ref, spread_ref):
    reduced = packed_ref[...]
    total = parts_ref[0]
    for block in range(1, parts_ref.shape[0]):
        total = total + parts_ref[block]
    reduced = reduced - total
    half = reduced.shape[1] // 2
    zero_ref[...] = reduced[:, :half]
    for target in range(spread_ref.shape[0]):
        spread_ref[target] = reduced[:, half:]


def weave(real, imag, conjugate):
    blocks = real.shape[1] // 128
    low = lax.broadcasted_iota(jnp.int32, (real.shape[0], 128), 1) < 64
    to_real, to_imag = [], []
    for block in range(blocks):
        lanes = slice(128 * block, 128 * (block + 1))
        re, im = real[:, lanes], imag[:, lanes]
        re_turned, im_turned = pltpu.roll(re, 64, 1), pltpu.roll(im, 64, 1)
        if conjugate:
            to_real += [jnp.where(low, re, im_turned), jnp.where(low, re_turned, im)]
            to_imag += [jnp.where(low, -im, re_turned), jnp.where(low, -im_turned, re)]
        else:
            to_real += [jnp.where(low, re, -im_turned), jnp.where(low, re_turned, -im)]
            to_imag += [jnp.where(low, im, re_turned), jnp.where(low, im_turned, re)]
    return jnp.concatenate([jnp.concatenate(to_real, axis=1), jnp.concatenate(to_imag, axis=1)], axis=0)


def apply_mat(gathered_ref, real, imag, conjugate):
    left = jnp.concatenate([gathered_ref[block] for block in range(gathered_ref.shape[0])], axis=1)
    return dot_split(left, weave(real, imag, conjugate))


def masked(start_ref, mat_ref):
    shape = mat_ref.shape[-2:]
    row_ids = lax.broadcasted_iota(jnp.int32, shape, 0) + start_ref[0]
    upper = lax.broadcasted_iota(jnp.int32, shape, 1) >= row_ids
    return jnp.where(upper, mat_ref[0, 0], 0.0), jnp.where(upper, mat_ref[1, 0], 0.0)


def spread(out_ref, value):
    for target in range(out_ref.shape[0]):
        out_ref[target] = value


def one_kernel(start_ref, gathered_ref, inv_ref, one_ref, spread_ref):
    real, imag = masked(start_ref, inv_ref)
    one = apply_mat(gathered_ref, real, imag, False)
    one_ref[...] = one
    spread(spread_ref, one)


def coupling_kernel(gathered_ref, couple_ref, zero_ref, spread_ref):
    coupling = apply_mat(gathered_ref, couple_ref[0], couple_ref[1], True)
    spread(spread_ref, zero_ref[...] - coupling)


def zero_kernel(start_ref, gathered_ref, inv_ref, one_ref, out_ref):
    real, imag = masked(start_ref, inv_ref)
    zero = apply_mat(gathered_ref, real, imag, False)
    one = one_ref[...]
    width = out_ref.shape[3]
    for part in range(2):
        lanes = slice(part * width, (part + 1) * width)
        out_ref[part, :, 0, :] = zero[:, lanes]
        out_ref[part, :, 1, :] = one[:, lanes]


SMEM = pl.BlockSpec(memory_space=pltpu.SMEM)


def call(kernel, out_shape, in_specs, *args):
    return pl.pallas_call(
        kernel,
        grid=(1,),
        in_specs=in_specs,
        out_specs=jax.tree.map(full, out_shape),
        out_shape=out_shape,
        compiler_params=pltpu.CompilerParams(vmem_limit_bytes=VMEM_LIMIT),
    )(*args)


def full(array):
    rank = len(array.shape)
    return pl.BlockSpec(array.shape, lambda step: (0,) * rank)


def panel_of(array, panel):
    return pl.BlockSpec((2, 1) + array.shape[2:], lambda step: (0, panel, 0, 0))


def per_device(x_done, l_below, rhs_window, inv_diag, l_couple):
    columns = lax.axis_size("pcol")
    side_blocks = lax.axis_size("prow")
    rows, width = rhs_window.shape[1], l_below.shape[2]
    core = (lax.axis_index("prow") % 2).astype(jnp.int32).reshape(1)
    start = (lax.axis_index("pcol") * width).astype(jnp.int32).reshape(1)
    keep, send, packed = update(core, x_done, l_below, rhs_window)
    pair = [(i, i ^ 1) for i in range(side_blocks)]
    summed = keep + lax.ppermute(send, "prow", pair)
    levels = [[2 * z + k for z in range(side_blocks // 2)] for k in range(2)]
    parts = lax.all_to_all(summed, "prow", 0, 0, axis_index_groups=levels)
    flat = jax.ShapeDtypeStruct((rows, 2 * width), F32)
    wide = jax.ShapeDtypeStruct((columns, rows, 2 * width), F32)
    gather = lambda array: lax.all_to_all(array, "pcol", 0, 0)
    reduced_zero, to_send = call(reduce_kernel, [flat, wide], [full(parts), full(packed)], parts, packed)
    one, to_send = call(
        one_kernel, [flat, wide], [SMEM, full(wide), panel_of(inv_diag, 1)], start, gather(to_send), inv_diag
    )
    to_send = call(
        coupling_kernel, wide, [full(wide), full(l_couple), full(flat)], gather(to_send), l_couple, reduced_zero
    )
    return call(
        zero_kernel,
        jax.ShapeDtypeStruct(rhs_window.shape, F32),
        [SMEM, full(wide), panel_of(inv_diag, 0), full(flat)],
        start, gather(to_send), inv_diag, one,
    )


def solution(mesh):
    placed = (
        P(None, None, "prow"),
        P(None, None, "pcol", "prow"),
        P(None, "prow", None, "pcol"),
        P(None, None, "pcol", None),
        P(None, "pcol", None),
    )
    return jax.shard_map(
        per_device,
        mesh=mesh,
        in_specs=placed,
        out_specs=P(None, "prow", None, "pcol"),
        check_vma=False,
    )
```

```python
import jax
import jax.numpy as jnp
from jax import lax
from jax.experimental import pallas as pl
from jax.experimental.pallas import tpu as pltpu
from jax.sharding import PartitionSpec as P

BF = jnp.bfloat16
F32 = jnp.float32
CHUNKS = 4
VMEM_LIMIT = 16 * 1024 * 1024
UPDATE_VMEM = 53 * 1024 * 1024
VMEM = pl.BlockSpec(memory_space=pltpu.VMEM)


def split(mat):
    high = mat.astype(BF)
    return high, (mat - high.astype(F32)).astype(BF)


def dot_split(left, right):
    left_high, left_low = split(left)
    right_high, right_low = split(right)
    return lax.dot_general(
        jnp.concatenate([left_high, left_low, left_high], axis=1),
        jnp.concatenate([right_high, right_high, right_low], axis=1),
        (((1,), (1,)), ((), ())),
        preferred_element_type=F32,
    )


def update_kernel(x_hbm, l_hbm, keep_ref, send_ref, x_buf, l_buf, total, sems):
    chunk = x_buf.shape[3]

    def copies(step):
        lanes = pl.ds(pl.multiple_of(step * chunk, chunk), chunk)
        return (
            pltpu.make_async_copy(l_hbm.at[:, :, :, lanes], l_buf.at[step], sems.at[step, 0]),
            pltpu.make_async_copy(x_hbm.at[:, :, lanes], x_buf.at[step], sems.at[step, 1]),
        )

    def begin(step, carry):
        for copy in copies(step):
            copy.start()
        return carry

    def multiply(step, carry):
        for copy in copies(step):
            copy.wait()
        left = jnp.concatenate([x_buf[step, 0], x_buf[step, 1]], axis=1)
        rows = []
        for panel in range(2):
            real, imag = l_buf[step, 0, panel], l_buf[step, 1, panel]
            rows.append(jnp.concatenate([real, imag], axis=1))
            rows.append(jnp.concatenate([-imag, real], axis=1))
        total[...] += dot_split(left, jnp.concatenate(rows, axis=0))
        return carry

    lax.fori_loop(0, CHUNKS, begin, 0)
    total[...] = jnp.zeros_like(total)
    lax.fori_loop(0, CHUNKS, multiply, 0)
    core = lax.axis_index("prow") % 2
    blocks, rows_each = keep_ref.shape[0], keep_ref.shape[1]
    for block in range(blocks):
        base = 2 * rows_each * block
        keep_ref[block] = total[pl.ds(pl.multiple_of(base + core * rows_each, 8), rows_each), :]
        send_ref[block] = total[pl.ds(pl.multiple_of(base + (1 - core) * rows_each, 8), rows_each), :]


def update(x_done, l_below, rows):
    _, sides, depth = x_done.shape
    width = l_below.shape[2]
    blocks = sides // (2 * rows)
    chunk = depth // CHUNKS
    half = jax.ShapeDtypeStruct((blocks, rows, 4 * width), F32)
    return pl.pallas_call(
        update_kernel,
        in_specs=[pl.BlockSpec(memory_space=pltpu.HBM)] * 2,
        out_specs=[VMEM] * 2,
        out_shape=[half, half],
        scratch_shapes=[
            pltpu.VMEM((CHUNKS, 2, sides, chunk), F32),
            pltpu.VMEM((CHUNKS, 2, 2, width, chunk), F32),
            pltpu.VMEM((sides, 4 * width), F32),
            pltpu.SemaphoreType.DMA((CHUNKS, 2)),
        ],
        compiler_params=pltpu.CompilerParams(vmem_limit_bytes=UPDATE_VMEM),
        cost_estimate=pl.CostEstimate(
            flops=2 * 3 * sides * 2 * depth * 4 * width, bytes_accessed=x_done.size * 4 + l_below.size * 4, transcendentals=0
        ),
    )(x_done, l_below)


def reduce_kernel(parts_ref, rhs_ref, zero_ref, spread_ref):
    rhs = jnp.concatenate([rhs_ref[part, :, panel, :] for panel in range(2) for part in range(2)], axis=1)
    total = parts_ref[0]
    for block in range(1, parts_ref.shape[0]):
        total = total + parts_ref[block]
    reduced = rhs - total
    half = reduced.shape[1] // 2
    zero_ref[...] = reduced[:, :half]
    spread(spread_ref, reduced[:, half:])


def weave(real, imag, conjugate):
    blocks = real.shape[1] // 128
    low = lax.broadcasted_iota(jnp.int32, (real.shape[0], 128), 1) < 64
    to_real, to_imag = [], []
    for block in range(blocks):
        lanes = slice(128 * block, 128 * (block + 1))
        re, im = real[:, lanes], imag[:, lanes]
        re_turned, im_turned = pltpu.roll(re, 64, 1), pltpu.roll(im, 64, 1)
        if conjugate:
            to_real += [jnp.where(low, re, im_turned), jnp.where(low, re_turned, im)]
            to_imag += [jnp.where(low, -im, re_turned), jnp.where(low, -im_turned, re)]
        else:
            to_real += [jnp.where(low, re, -im_turned), jnp.where(low, re_turned, -im)]
            to_imag += [jnp.where(low, im, re_turned), jnp.where(low, im_turned, re)]
    return jnp.concatenate([jnp.concatenate(to_real, axis=1), jnp.concatenate(to_imag, axis=1)], axis=0)


def apply_mat(gathered_ref, mat_ref):
    depth = mat_ref.shape[0] // 2
    high, low = split(jnp.concatenate([gathered_ref[block] for block in range(gathered_ref.shape[0])], axis=1))
    rows = high.shape[0]
    both = jnp.dot(jnp.concatenate([high, low], axis=0), mat_ref[:depth, :], preferred_element_type=F32)
    return both[:rows] + both[rows:] + jnp.dot(high, mat_ref[depth:, :], preferred_element_type=F32)


def store_split(out_ref, mat):
    depth = mat.shape[1]
    out_ref[:depth, :], out_ref[depth:, :] = split(mat.T)


def prepare_kernel(inv_ref, couple_ref, keep_ref, one_ref, coupling_ref, zero_ref, kept_ref):
    del keep_ref, kept_ref
    store_split(one_ref, weave(*masked(inv_ref, 1), False))
    store_split(coupling_ref, weave(couple_ref[0], couple_ref[1], True))
    store_split(zero_ref, weave(*masked(inv_ref, 0), False))


def masked(inv_ref, panel):
    shape = inv_ref.shape[2:]
    row_ids = lax.broadcasted_iota(jnp.int32, shape, 0) + lax.axis_index("pcol") * shape[0]
    upper = lax.broadcasted_iota(jnp.int32, shape, 1) >= row_ids
    return jnp.where(upper, inv_ref[0, panel], 0.0), jnp.where(upper, inv_ref[1, panel], 0.0)


def spread(out_ref, value):
    for target in range(out_ref.shape[0]):
        out_ref[target] = value


def one_kernel(gathered_ref, mat_ref, one_ref, spread_ref):
    one = apply_mat(gathered_ref, mat_ref)
    one_ref[...] = one
    spread(spread_ref, one)


def coupling_kernel(gathered_ref, mat_ref, zero_ref, spread_ref):
    spread(spread_ref, zero_ref[...] - apply_mat(gathered_ref, mat_ref))


def zero_kernel(gathered_ref, mat_ref, one_ref, out_ref):
    zero = apply_mat(gathered_ref, mat_ref)
    one = one_ref[...]
    width = out_ref.shape[3]
    for part in range(2):
        lanes = slice(part * width, (part + 1) * width)
        out_ref[part, :, 0, :] = zero[:, lanes]
        out_ref[part, :, 1, :] = one[:, lanes]


def call(kernel, out_shape, *args, out_spec=VMEM):
    return pl.pallas_call(
        kernel,
        in_specs=[VMEM] * len(args),
        out_specs=jax.tree.map(lambda array: out_spec, out_shape),
        out_shape=out_shape,
        compiler_params=pltpu.CompilerParams(vmem_limit_bytes=VMEM_LIMIT),
    )(*args)


def per_device(x_done, l_below, rhs_window, inv_diag, l_couple):
    columns = lax.axis_size("pcol")
    side_blocks = lax.axis_size("prow")
    rows, width = rhs_window.shape[1], l_below.shape[2]
    keep, send = update(x_done, l_below, rows)
    pair = [(i, i ^ 1) for i in range(side_blocks)]
    received = lax.ppermute(send, "prow", pair)
    mat = jax.ShapeDtypeStruct((4 * columns * width, 2 * width), BF)
    one_mat, coupling_mat, zero_mat, keep = pl.pallas_call(
        prepare_kernel,
        in_specs=[VMEM] * 3,
        out_specs=[VMEM] * 4,
        out_shape=[mat] * 3 + [jax.ShapeDtypeStruct(keep.shape, F32)],
        input_output_aliases={2: 3},
        compiler_params=pltpu.CompilerParams(vmem_limit_bytes=VMEM_LIMIT),
    )(inv_diag, l_couple, keep)
    levels = [[2 * z + k for z in range(side_blocks // 2)] for k in range(2)]
    parts = lax.all_to_all(keep + received, "prow", 0, 0, axis_index_groups=levels)
    flat = jax.ShapeDtypeStruct((rows, 2 * width), F32)
    wide = jax.ShapeDtypeStruct((columns, rows, 2 * width), F32)
    gather = lambda array: lax.all_to_all(array, "pcol", 0, 0)
    reduced_zero, to_send = call(reduce_kernel, [flat, wide], parts, rhs_window)
    one, to_send = call(one_kernel, [flat, wide], gather(to_send), one_mat)
    to_send = call(coupling_kernel, wide, gather(to_send), coupling_mat, reduced_zero)
    return call(zero_kernel, jax.ShapeDtypeStruct(rhs_window.shape, F32), gather(to_send), zero_mat, one)


def solution(mesh):
    placed = (
        P(None, None, "prow"),
        P(None, None, "pcol", "prow"),
        P(None, "prow", None, "pcol"),
        P(None, None, "pcol", None),
        P(None, "pcol", None),
    )
    return jax.shard_map(
        per_device,
        mesh=mesh,
        in_specs=placed,
        out_specs=P(None, "prow", None, "pcol"),
        check_vma=False,
    )
```

```python
import jax
import jax.numpy as jnp
from jax import lax
from jax.experimental import pallas as pl
from jax.experimental.pallas import tpu as pltpu
from jax.sharding import PartitionSpec as P

BF = jnp.bfloat16
F32 = jnp.float32
CHUNKS = 4
VMEM_LIMIT = 16 * 1024 * 1024
UPDATE_VMEM = 53 * 1024 * 1024
VMEM = pl.BlockSpec(memory_space=pltpu.VMEM)


def split(mat):
    high = mat.astype(BF)
    return high, (mat - high.astype(F32)).astype(BF)


def dot_split(left, right):
    left_high, left_low = split(left)
    right_high, right_low = split(right)
    return lax.dot_general(
        jnp.concatenate([left_high, left_low, left_high], axis=1),
        jnp.concatenate([right_high, right_high, right_low], axis=1),
        (((1,), (1,)), ((), ())),
        preferred_element_type=F32,
    )


def update_kernel(x_hbm, l_hbm, out_ref, x_buf, l_buf, total, sems):
    chunk = x_buf.shape[3]

    def copies(step):
        lanes = pl.ds(pl.multiple_of(step * chunk, chunk), chunk)
        return (
            pltpu.make_async_copy(l_hbm.at[:, :, :, lanes], l_buf.at[step], sems.at[step, 0]),
            pltpu.make_async_copy(x_hbm.at[:, :, lanes], x_buf.at[step], sems.at[step, 1]),
        )

    def begin(step, carry):
        for copy in copies(step):
            copy.start()
        return carry

    def multiply(step, carry):
        for copy in copies(step):
            copy.wait()
        left = jnp.concatenate([x_buf[step, 0], x_buf[step, 1]], axis=1)
        rows = []
        for panel in range(2):
            real, imag = l_buf[step, 0, panel], l_buf[step, 1, panel]
            rows.append(jnp.concatenate([real, imag], axis=1))
            rows.append(jnp.concatenate([-imag, real], axis=1))
        total[...] += dot_split(left, jnp.concatenate(rows, axis=0))
        return carry

    lax.fori_loop(0, CHUNKS, begin, 0)
    total[...] = jnp.zeros_like(total)
    lax.fori_loop(0, CHUNKS, multiply, 0)
    for level in range(out_ref.shape[0]):
        out_ref[level] = total[level * out_ref.shape[1] : (level + 1) * out_ref.shape[1], :]


def update(x_done, l_below, rows):
    _, sides, depth = x_done.shape
    width = l_below.shape[2]
    chunk = depth // CHUNKS
    return pl.pallas_call(
        update_kernel,
        in_specs=[pl.BlockSpec(memory_space=pltpu.HBM)] * 2,
        out_specs=VMEM,
        out_shape=jax.ShapeDtypeStruct((sides // rows, rows, 4 * width), F32),
        scratch_shapes=[
            pltpu.VMEM((CHUNKS, 2, sides, chunk), F32),
            pltpu.VMEM((CHUNKS, 2, 2, width, chunk), F32),
            pltpu.VMEM((sides, 4 * width), F32),
            pltpu.SemaphoreType.DMA((CHUNKS, 2)),
        ],
        compiler_params=pltpu.CompilerParams(vmem_limit_bytes=UPDATE_VMEM),
        cost_estimate=pl.CostEstimate(
            flops=2 * 3 * sides * 2 * depth * 4 * width, bytes_accessed=x_done.size * 4 + l_below.size * 4, transcendentals=0
        ),
    )(x_done, l_below)


def subtract_kernel(rhs_ref, total_ref, out_ref):
    del total_ref
    rows = rhs_ref.shape[1]
    rhs = jnp.concatenate([rhs_ref[part, :, panel, :] for panel in range(2) for part in range(2)], axis=1)
    device = lax.axis_index("prow")
    own = pl.ds(pl.multiple_of(device % 2 * rows, rows), rows)
    out_ref[device // 2, own, :] -= rhs


def add_kernel(mine_ref, other_ref, out_ref):
    del mine_ref
    out_ref[...] += other_ref[...]


def reduce_kernel(parts_ref, spread_ref):
    total = parts_ref[0]
    for block in range(1, parts_ref.shape[0]):
        total = total + parts_ref[block]
    spread(spread_ref, -total)


def weave(real, imag):
    blocks = real.shape[1] // 128
    low = lax.broadcasted_iota(jnp.int32, (real.shape[0], 128), 1) < 64
    to_real, to_imag = [], []
    for block in range(blocks):
        lanes = slice(128 * block, 128 * (block + 1))
        re, im = real[:, lanes], imag[:, lanes]
        re_turned, im_turned = pltpu.roll(re, 64, 1), pltpu.roll(im, 64, 1)
        to_real += [jnp.where(low, re, -im_turned), jnp.where(low, re_turned, -im)]
        to_imag += [jnp.where(low, im, re_turned), jnp.where(low, im_turned, re)]
    return jnp.concatenate([jnp.concatenate(to_real, axis=1), jnp.concatenate(to_imag, axis=1)], axis=0)


def apply_mat(gathered_ref, lanes, mat_high, mat_low):
    blocks = [gathered_ref[block, :, lanes] for block in range(gathered_ref.shape[0])]
    high, low = split(jnp.concatenate(blocks, axis=1))
    rows = high.shape[0]
    both = jnp.dot(jnp.concatenate([high, low], axis=0), mat_high, preferred_element_type=F32)
    return both[:rows] + both[rows:] + jnp.dot(high, mat_low, preferred_element_type=F32)


def masked(inv_ref, panel):
    shape = inv_ref.shape[2:]
    row_ids = lax.broadcasted_iota(jnp.int32, shape, 0) + lax.axis_index("pcol") * shape[0]
    upper = lax.broadcasted_iota(jnp.int32, shape, 1) >= row_ids
    return jnp.where(upper, inv_ref[0, panel], 0.0), jnp.where(upper, inv_ref[1, panel], 0.0)


def spread(out_ref, value):
    for target in range(out_ref.shape[0]):
        out_ref[target] = value


def blank(out_ref):
    out_ref[0] = jnp.zeros(out_ref.shape[1:], F32)


def woven(real, imag):
    return split(weave(real, imag).T)


def one_kernel(gathered_ref, inv_ref, ship_ref, held_ref, blank_ref):
    blank(blank_ref)
    half, rows = gathered_ref.shape[2] // 2, held_ref.shape[1]
    for place, panel in enumerate((0, 1)):
        lanes = slice(panel * half, (panel + 1) * half)
        applied = apply_mat(gathered_ref, lanes, *woven(*masked(inv_ref, panel)))
        ship_ref[place], held_ref[place] = applied[:rows], applied[rows:]


def spread_kernel(mine_ref, other_ref, own_ref, spread_ref):
    own = jnp.where(lax.axis_index("prow") % 2 == 1, mine_ref[...], other_ref[...])
    own_ref[...] = own
    spread(spread_ref, own[1])


def columns_kernel(couple_ref, after_ref, spread_ref):
    del after_ref
    width = spread_ref.shape[3]
    lanes = pl.ds(pl.multiple_of(lax.axis_index("prow") // 2 * width, width), width)
    for target in range(spread_ref.shape[0]):
        spread_ref[target] = couple_ref[:, :, lanes]


def product_kernel(inv_ref, columns_ref, spread_ref, ship_ref, held_ref):
    blank(ship_ref)
    blank(held_ref)
    left = jnp.concatenate(masked(inv_ref, 0), axis=0)
    count, rows = columns_ref.shape[0], left.shape[0] // 2
    right = jnp.concatenate(
        [jnp.concatenate([columns_ref[block, part] for block in range(count)], axis=0) for part in range(2)], axis=1
    )
    left_high, left_low = split(left)
    right_high, right_low = split(right)
    both = jnp.dot(jnp.concatenate([left_high, left_low], axis=0), right_high, preferred_element_type=F32)
    product = both[: 2 * rows] + both[2 * rows :] + jnp.dot(left_high, right_low, preferred_element_type=F32)
    half = product.shape[1] // 2
    for target in range(spread_ref.shape[0]):
        spread_ref[target, 0] = product[:rows, :half] + product[rows:, half:]
        spread_ref[target, 1] = product[rows:, :half] - product[:rows, half:]


def zero_kernel(gathered_ref, mine_ref, other_ref, own_ref, out_ref):
    upper = lax.axis_index("prow") % 2 == 1
    product = jnp.where(upper, other_ref[...], mine_ref[...])
    levels, width = product.shape[0] // 2, out_ref.shape[3]
    real = jnp.concatenate([product[2 * level] for level in range(levels)], axis=1)
    imag = jnp.concatenate([product[2 * level + 1] for level in range(levels)], axis=1)
    zero = own_ref[0] - apply_mat(gathered_ref, slice(None), *woven(real, imag))
    for panel, solved in enumerate((zero, own_ref[1])):
        for part in range(2):
            out_ref[part, :, panel, :] = solved[:, part * width : (part + 1) * width]


def blank_kernel(after_ref, out_ref):
    del after_ref
    blank(out_ref)


def call(kernel, out_shape, *args, aliases={}):
    return pl.pallas_call(
        kernel,
        in_specs=[VMEM] * len(args),
        out_specs=jax.tree.map(lambda array: VMEM, out_shape),
        out_shape=out_shape,
        input_output_aliases=aliases,
        compiler_params=pltpu.CompilerParams(vmem_limit_bytes=VMEM_LIMIT),
    )(*args)


def per_device(x_done, l_below, rhs_window, inv_diag, l_couple):
    columns, levels = lax.axis_size("pcol"), lax.axis_size("prow") // 2
    rows, width = 2 * rhs_window.shape[1], l_below.shape[2]
    block = inv_diag.shape[3] // levels
    upper = lax.axis_index("prow") % 2 == 1
    swap = [(device, device ^ 1) for device in range(2 * levels)]
    same_core = [[2 * level + core for level in range(levels)] for core in range(2)]
    array = lambda *shape: jax.ShapeDtypeStruct(shape, F32)
    over_columns = lambda value: lax.all_to_all(value, "pcol", 0, 0)
    over_levels = lambda value: lax.all_to_all(value, "prow", 0, 0, axis_index_groups=same_core)

    total = update(x_done, l_below, rows)
    total = call(subtract_kernel, array(*total.shape), rhs_window, total, aliases={1: 0})
    received = lax.ppermute(total, "prow", swap)
    parts = array(columns, 2, width, block)

    share = lambda l_couple, after: over_columns(call(columns_kernel, parts, l_couple, after))
    skip = lambda l_couple, after: call(blank_kernel, parts, after)
    gathered = lax.cond(upper, skip, share, l_couple, total)
    summed = call(add_kernel, array(*total.shape), total, received, aliases={0: 0})
    own = array(2, rows // 2, 2 * width)
    whole = array(columns, rows, 2 * width)

    def solve(summed, inv_diag, gathered):
        del gathered
        reduced = call(reduce_kernel, array(columns, rows, 4 * width), over_levels(summed))
        return tuple(call(one_kernel, [own, own, whole], over_columns(reduced), inv_diag))

    def multiply(summed, inv_diag, gathered):
        del summed
        product = array(levels, 2, width, block)
        product, ship, held = call(product_kernel, [product, own, own], inv_diag, gathered)
        return ship, held, over_levels(product).reshape(whole.shape)

    ship, held, product = lax.cond(upper, solve, multiply, summed, inv_diag, gathered)
    shipped = lax.ppermute(ship, "prow", swap)
    other = lax.ppermute(product, "prow", swap)
    held, one = call(spread_kernel, [own, array(columns, rows // 2, 2 * width)], held, shipped)
    return call(zero_kernel, array(*rhs_window.shape), over_columns(one), product, other, held)


def solution(mesh):
    placed = (
        P(None, None, "prow"),
        P(None, None, "pcol", "prow"),
        P(None, "prow", None, "pcol"),
        P(None, None, "pcol", None),
        P(None, "pcol", None),
    )
    return jax.shard_map(
        per_device,
        mesh=mesh,
        in_specs=placed,
        out_specs=P(None, "prow", None, "pcol"),
        check_vma=False,
    )
```

```python
import jax
import jax.numpy as jnp
from jax import lax
from jax.experimental import pallas as pl
from jax.experimental.pallas import tpu as pltpu
from jax.sharding import PartitionSpec as P

BF = jnp.bfloat16
F32 = jnp.float32
CHUNKS = 4
VMEM_LIMIT = 16 * 1024 * 1024
UPDATE_VMEM = 53 * 1024 * 1024
VMEM = pl.BlockSpec(memory_space=pltpu.VMEM)


def split(mat):
    high = mat.astype(BF)
    return high, (mat - high.astype(F32)).astype(BF)


def dot_split(left, right):
    left_high, left_low = split(left)
    right_high, right_low = split(right)
    return lax.dot_general(
        jnp.concatenate([left_high, left_low, left_high], axis=1),
        jnp.concatenate([right_high, right_high, right_low], axis=1),
        (((1,), (1,)), ((), ())),
        preferred_element_type=F32,
    )


def update_kernel(x_hbm, l_hbm, out_ref, x_buf, l_buf, total, sems):
    chunk = x_buf.shape[3]

    def copies(step):
        lanes = pl.ds(pl.multiple_of(step * chunk, chunk), chunk)
        return (
            pltpu.make_async_copy(l_hbm.at[:, :, :, lanes], l_buf.at[step], sems.at[step, 0]),
            pltpu.make_async_copy(x_hbm.at[:, :, lanes], x_buf.at[step], sems.at[step, 1]),
        )

    def begin(step, carry):
        for copy in copies(step):
            copy.start()
        return carry

    def multiply(step, carry):
        for copy in copies(step):
            copy.wait()
        left = jnp.concatenate([x_buf[step, 0], x_buf[step, 1]], axis=1)
        rows = []
        for panel in range(2):
            real, imag = l_buf[step, 0, panel], l_buf[step, 1, panel]
            rows.append(jnp.concatenate([real, imag], axis=1))
            rows.append(jnp.concatenate([-imag, real], axis=1))
        total[...] += dot_split(left, jnp.concatenate(rows, axis=0))
        return carry

    lax.fori_loop(0, CHUNKS, begin, 0)
    total[...] = jnp.zeros_like(total)
    lax.fori_loop(0, CHUNKS, multiply, 0)
    for level in range(out_ref.shape[0]):
        out_ref[level] = total[level * out_ref.shape[1] : (level + 1) * out_ref.shape[1], :]


def update(x_done, l_below, rows):
    _, sides, depth = x_done.shape
    width = l_below.shape[2]
    chunk = depth // CHUNKS
    return pl.pallas_call(
        update_kernel,
        in_specs=[pl.BlockSpec(memory_space=pltpu.HBM)] * 2,
        out_specs=VMEM,
        out_shape=jax.ShapeDtypeStruct((sides // rows, rows, 4 * width), F32),
        scratch_shapes=[
            pltpu.VMEM((CHUNKS, 2, sides, chunk), F32),
            pltpu.VMEM((CHUNKS, 2, 2, width, chunk), F32),
            pltpu.VMEM((sides, 4 * width), F32),
            pltpu.SemaphoreType.DMA((CHUNKS, 2)),
        ],
        compiler_params=pltpu.CompilerParams(vmem_limit_bytes=UPDATE_VMEM),
        cost_estimate=pl.CostEstimate(
            flops=2 * 3 * sides * 2 * depth * 4 * width, bytes_accessed=x_done.size * 4 + l_below.size * 4, transcendentals=0
        ),
    )(x_done, l_below)


def subtract_kernel(rhs_ref, total_ref, out_ref):
    del total_ref
    rows = rhs_ref.shape[1]
    rhs = jnp.concatenate([rhs_ref[part, :, panel, :] for panel in range(2) for part in range(2)], axis=1)
    device = lax.axis_index("prow")
    own = pl.ds(pl.multiple_of(device % 2 * rows, rows), rows)
    out_ref[device // 2, own, :] -= rhs


def add_kernel(mine_ref, other_ref, out_ref):
    del mine_ref
    out_ref[...] += other_ref[...]


def reduce_kernel(parts_ref, spread_ref):
    total = parts_ref[0]
    for block in range(1, parts_ref.shape[0]):
        total = total + parts_ref[block]
    spread(spread_ref, -total)


def weave(real, imag):
    blocks = real.shape[1] // 128
    low = lax.broadcasted_iota(jnp.int32, (real.shape[0], 128), 1) < 64
    to_real, to_imag = [], []
    for block in range(blocks):
        lanes = slice(128 * block, 128 * (block + 1))
        re, im = real[:, lanes], imag[:, lanes]
        re_turned, im_turned = pltpu.roll(re, 64, 1), pltpu.roll(im, 64, 1)
        to_real += [jnp.where(low, re, -im_turned), jnp.where(low, re_turned, -im)]
        to_imag += [jnp.where(low, im, re_turned), jnp.where(low, im_turned, re)]
    return jnp.concatenate([jnp.concatenate(to_real, axis=1), jnp.concatenate(to_imag, axis=1)], axis=0)


def apply_mat(gathered_ref, lanes, mat_high, mat_low):
    blocks = [gathered_ref[block, :, lanes] for block in range(gathered_ref.shape[0])]
    high, low = split(jnp.concatenate(blocks, axis=1))
    rows = high.shape[0]
    both = jnp.dot(jnp.concatenate([high, low], axis=0), mat_high, preferred_element_type=F32)
    return both[:rows] + both[rows:] + jnp.dot(high, mat_low, preferred_element_type=F32)


def masked(inv_ref, panel):
    shape = inv_ref.shape[2:]
    row_ids = lax.broadcasted_iota(jnp.int32, shape, 0) + lax.axis_index("pcol") * shape[0]
    upper = lax.broadcasted_iota(jnp.int32, shape, 1) >= row_ids
    return jnp.where(upper, inv_ref[0, panel], 0.0), jnp.where(upper, inv_ref[1, panel], 0.0)


def spread(out_ref, value):
    for target in range(out_ref.shape[0]):
        out_ref[target] = value


def blank(out_ref):
    out_ref[0] = jnp.zeros(out_ref.shape[1:], F32)


def woven(real, imag):
    return split(weave(real, imag).T)


def ready_kernel(inv_ref, after_ref, out_ref):
    del after_ref
    mat = weave(*masked(inv_ref, 1)).T
    count = mat.shape[0] // out_ref.shape[0]
    for block in range(out_ref.shape[0]):
        out_ref[block] = mat[block * count : (block + 1) * count]


def one_kernel(gathered_ref, ready_ref, inv_ref, ship_ref, held_ref, blank_ref):
    blank(blank_ref)
    half, rows = gathered_ref.shape[2] // 2, held_ref.shape[1]
    ready = jnp.concatenate([ready_ref[block] for block in range(ready_ref.shape[0])], axis=0)
    for panel, mats in enumerate((woven(*masked(inv_ref, 0)), split(ready))):
        applied = apply_mat(gathered_ref, slice(panel * half, (panel + 1) * half), *mats)
        ship_ref[panel], held_ref[panel] = applied[:rows], applied[rows:]


def spread_kernel(mine_ref, other_ref, product_ref, own_ref, spread_ref, kept_ref):
    del product_ref, kept_ref
    own = jnp.where(lax.axis_index("prow") % 2 == 1, mine_ref[...], other_ref[...])
    own_ref[...] = own
    spread(spread_ref, own[1])


def columns_kernel(couple_ref, after_ref, spread_ref):
    del after_ref
    width = spread_ref.shape[2]
    lanes = pl.ds(pl.multiple_of(lax.axis_index("prow") // 2 * width, width), width)
    both = jnp.concatenate([couple_ref[0, :, lanes], couple_ref[1, :, lanes]], axis=0)
    spread(spread_ref, both)


def product_kernel(inv_ref, columns_ref, spread_ref, ship_ref, held_ref):
    blank(ship_ref)
    blank(held_ref)
    left = jnp.concatenate(masked(inv_ref, 0), axis=0)
    count, rows = columns_ref.shape[0], left.shape[0] // 2
    right = jnp.concatenate(
        [
            jnp.concatenate([columns_ref[block, part * rows : (part + 1) * rows] for block in range(count)], axis=0)
            for part in range(2)
        ],
        axis=1,
    )
    left_high, left_low = split(left)
    right_high, right_low = split(right)
    both = jnp.dot(jnp.concatenate([left_high, left_low], axis=0), right_high, preferred_element_type=F32)
    product = both[: 2 * rows] + both[2 * rows :] + jnp.dot(left_high, right_low, preferred_element_type=F32)
    half = product.shape[1] // 2
    for target in range(spread_ref.shape[0]):
        spread_ref[target, 0] = product[:rows, :half] + product[rows:, half:]
        spread_ref[target, 1] = product[rows:, :half] - product[:rows, half:]


def product_mats(product_ref):
    levels = product_ref.shape[0] // 2
    real = jnp.concatenate([product_ref[2 * level] for level in range(levels)], axis=1)
    imag = jnp.concatenate([product_ref[2 * level + 1] for level in range(levels)], axis=1)
    return woven(real, imag)


def weave_kernel(product_ref, mat_ref):
    depth = mat_ref.shape[0] // 2
    mat_ref[:depth, :], mat_ref[depth:, :] = product_mats(product_ref)


def zero_kernel(gathered_ref, mat_ref, other_ref, own_ref, out_ref):
    upper = lax.axis_index("prow") % 2 == 1
    depth, width = mat_ref.shape[0] // 2, out_ref.shape[3]

    def finish(mat_high, mat_low):
        zero = own_ref[0] - apply_mat(gathered_ref, slice(None), mat_high, mat_low)
        for panel, solved in enumerate((zero, own_ref[1])):
            for part in range(2):
                out_ref[part, :, panel, :] = solved[:, part * width : (part + 1) * width]

    @pl.when(upper)
    def _():
        finish(*product_mats(other_ref))

    @pl.when(jnp.logical_not(upper))
    def _():
        finish(mat_ref[:depth, :], mat_ref[depth:, :])


def call(kernel, out_shape, *args, aliases={}):
    return pl.pallas_call(
        kernel,
        in_specs=[VMEM] * len(args),
        out_specs=jax.tree.map(lambda array: VMEM, out_shape),
        out_shape=out_shape,
        input_output_aliases=aliases,
        compiler_params=pltpu.CompilerParams(vmem_limit_bytes=VMEM_LIMIT),
    )(*args)


def per_device(x_done, l_below, rhs_window, inv_diag, l_couple):
    columns, levels = lax.axis_size("pcol"), lax.axis_size("prow") // 2
    rows, width = 2 * rhs_window.shape[1], l_below.shape[2]
    block = inv_diag.shape[3] // levels
    upper = lax.axis_index("prow") % 2 == 1
    swap = [(device, device ^ 1) for device in range(2 * levels)]
    same_core = [[2 * level + core for level in range(levels)] for core in range(2)]
    array = lambda *shape: jax.ShapeDtypeStruct(shape, F32)
    over_columns = lambda value: lax.all_to_all(value, "pcol", 0, 0)
    over_levels = lambda value: lax.all_to_all(value, "prow", 0, 0, axis_index_groups=same_core)

    total = update(x_done, l_below, rows)
    total = call(subtract_kernel, array(*total.shape), rhs_window, total, aliases={1: 0})
    received = lax.ppermute(total, "prow", swap)
    parts = array(columns, 2 * width, block)

    share = lambda l_couple, inv_diag, after: over_columns(call(columns_kernel, parts, l_couple, after))
    ready = lambda l_couple, inv_diag, after: call(ready_kernel, parts, inv_diag, after)
    gathered = lax.cond(upper, ready, share, l_couple, inv_diag, total)
    summed = call(add_kernel, array(*total.shape), total, received, aliases={0: 0})
    own = array(2, rows // 2, 2 * width)
    whole = array(columns, rows, 2 * width)

    def solve(summed, inv_diag, ready):
        reduced = call(reduce_kernel, array(columns, rows, 4 * width), over_levels(summed))
        return tuple(call(one_kernel, [own, own, whole], over_columns(reduced), ready, inv_diag))

    def multiply(summed, inv_diag, gathered):
        del summed
        product = array(levels, 2, width, block)
        product, ship, held = call(product_kernel, [product, own, own], inv_diag, gathered)
        return ship, held, over_levels(product).reshape(whole.shape)

    ship, held, product = lax.cond(upper, solve, multiply, summed, inv_diag, gathered)
    shipped = lax.ppermute(ship, "prow", swap)
    mat = jax.ShapeDtypeStruct((4 * columns * width, 2 * width), BF)
    mat = call(weave_kernel, mat, product)
    one = array(columns, rows // 2, 2 * width)
    held, one, product = call(spread_kernel, [own, one, whole], held, shipped, product, aliases={2: 2})
    other = lax.ppermute(product, "prow", swap)
    return call(zero_kernel, array(*rhs_window.shape), over_columns(one), mat, other, held)


def solution(mesh):
    placed = (
        P(None, None, "prow"),
        P(None, None, "pcol", "prow"),
        P(None, "prow", None, "pcol"),
        P(None, None, "pcol", None),
        P(None, "pcol", None),
    )
    return jax.shard_map(
        per_device,
        mesh=mesh,
        in_specs=placed,
        out_specs=P(None, "prow", None, "pcol"),
        check_vma=False,
    )
```

```python
import functools

import jax
import jax.numpy as jnp
from jax import lax
from jax.experimental import pallas as pl
from jax.experimental.pallas import tpu as pltpu
from jax.sharding import PartitionSpec as P

BF = jnp.bfloat16
F32 = jnp.float32
PLAN = ((2, 256), (3, 512))
VMEM_LIMIT = 16 * 1024 * 1024
UPDATE_VMEM = 53 * 1024 * 1024
VMEM = pl.BlockSpec(memory_space=pltpu.VMEM)


def split(mat):
    high = mat.astype(BF)
    return high, (mat - high.astype(F32)).astype(BF)


def dot_split(left, right):
    left_high, left_low = split(left)
    right_high, right_low = split(right)
    return lax.dot_general(
        jnp.concatenate([left_high, left_low, left_high], axis=1),
        jnp.concatenate([right_high, right_high, right_low], axis=1),
        (((1,), (1,)), ((), ())),
        preferred_element_type=F32,
    )


def update_kernel(x_hbm, l_hbm, out_ref, *scratch):
    groups = len(PLAN)
    x_bufs, l_bufs, (total, sems) = scratch[:groups], scratch[groups : 2 * groups], scratch[2 * groups :]

    def copies(group, step):
        count, width = PLAN[group]
        first = sum(other for other, _ in PLAN[:group])
        start = sum(other * wide for other, wide in PLAN[:group])
        lanes = pl.ds(pl.multiple_of(start + step * width, 128), width)
        return (
            pltpu.make_async_copy(l_hbm.at[:, :, :, lanes], l_bufs[group].at[step], sems.at[first + step, 0]),
            pltpu.make_async_copy(x_hbm.at[:, :, lanes], x_bufs[group].at[step], sems.at[first + step, 1]),
        )

    def begin(group, step, carry):
        for copy in copies(group, step):
            copy.start()
        return carry

    def multiply(group, step, carry):
        for copy in copies(group, step):
            copy.wait()
        x_buf, l_buf = x_bufs[group], l_bufs[group]
        left = jnp.concatenate([x_buf[step, 0], x_buf[step, 1]], axis=1)
        rows = []
        for panel in range(2):
            real, imag = l_buf[step, 0, panel], l_buf[step, 1, panel]
            rows.append(jnp.concatenate([real, imag], axis=1))
            rows.append(jnp.concatenate([-imag, real], axis=1))
        total[...] += dot_split(left, jnp.concatenate(rows, axis=0))
        return carry

    for group in range(groups):
        lax.fori_loop(0, PLAN[group][0], functools.partial(begin, group), 0)
    total[...] = jnp.zeros_like(total)
    for group in range(groups):
        lax.fori_loop(0, PLAN[group][0], functools.partial(multiply, group), 0)
    for level in range(out_ref.shape[0]):
        out_ref[level] = total[level * out_ref.shape[1] : (level + 1) * out_ref.shape[1], :]


def update(x_done, l_below, rows):
    _, sides, depth = x_done.shape
    width = l_below.shape[2]
    return pl.pallas_call(
        update_kernel,
        in_specs=[pl.BlockSpec(memory_space=pltpu.HBM)] * 2,
        out_specs=VMEM,
        out_shape=jax.ShapeDtypeStruct((sides // rows, rows, 4 * width), F32),
        scratch_shapes=[
            *(pltpu.VMEM((count, 2, sides, chunk), F32) for count, chunk in PLAN),
            *(pltpu.VMEM((count, 2, 2, width, chunk), F32) for count, chunk in PLAN),
            pltpu.VMEM((sides, 4 * width), F32),
            pltpu.SemaphoreType.DMA((sum(count for count, _ in PLAN), 2)),
        ],
        compiler_params=pltpu.CompilerParams(vmem_limit_bytes=UPDATE_VMEM),
        cost_estimate=pl.CostEstimate(
            flops=2 * 3 * sides * 2 * depth * 4 * width, bytes_accessed=x_done.size * 4 + l_below.size * 4, transcendentals=0
        ),
    )(x_done, l_below)


def subtract_kernel(rhs_ref, total_ref, out_ref):
    del total_ref
    rows = rhs_ref.shape[1]
    rhs = jnp.concatenate([rhs_ref[part, :, panel, :] for panel in range(2) for part in range(2)], axis=1)
    device = lax.axis_index("prow")
    own = pl.ds(pl.multiple_of(device % 2 * rows, rows), rows)
    out_ref[device // 2, own, :] -= rhs


def add_kernel(mine_ref, other_ref, out_ref):
    del mine_ref
    out_ref[...] += other_ref[...]


def reduce_kernel(parts_ref, spread_ref):
    total = parts_ref[0]
    for block in range(1, parts_ref.shape[0]):
        total = total + parts_ref[block]
    spread(spread_ref, -total)


def weave(real, imag):
    blocks = real.shape[1] // 128
    low = lax.broadcasted_iota(jnp.int32, (real.shape[0], 128), 1) < 64
    to_real, to_imag = [], []
    for block in range(blocks):
        lanes = slice(128 * block, 128 * (block + 1))
        re, im = real[:, lanes], imag[:, lanes]
        re_turned, im_turned = pltpu.roll(re, 64, 1), pltpu.roll(im, 64, 1)
        to_real += [jnp.where(low, re, -im_turned), jnp.where(low, re_turned, -im)]
        to_imag += [jnp.where(low, im, re_turned), jnp.where(low, im_turned, re)]
    return jnp.concatenate([jnp.concatenate(to_real, axis=1), jnp.concatenate(to_imag, axis=1)], axis=0)


def apply_mat(gathered_ref, lanes, mat_high, mat_low):
    blocks = [gathered_ref[block, :, lanes] for block in range(gathered_ref.shape[0])]
    high, low = split(jnp.concatenate(blocks, axis=1))
    rows = high.shape[0]
    both = jnp.dot(jnp.concatenate([high, low], axis=0), mat_high, preferred_element_type=F32)
    return both[:rows] + both[rows:] + jnp.dot(high, mat_low, preferred_element_type=F32)


def masked(inv_ref, panel):
    shape = inv_ref.shape[2:]
    row_ids = lax.broadcasted_iota(jnp.int32, shape, 0) + lax.axis_index("pcol") * shape[0]
    upper = lax.broadcasted_iota(jnp.int32, shape, 1) >= row_ids
    return jnp.where(upper, inv_ref[0, panel], 0.0), jnp.where(upper, inv_ref[1, panel], 0.0)


def spread(out_ref, value):
    for target in range(out_ref.shape[0]):
        out_ref[target] = value


def blank(out_ref):
    out_ref[0] = jnp.zeros(out_ref.shape[1:], F32)


def woven(real, imag):
    return split(weave(real, imag).T)


def ready_kernel(inv_ref, after_ref, out_ref):
    del after_ref
    mat = weave(*masked(inv_ref, 1)).T
    count = mat.shape[0] // out_ref.shape[0]
    for block in range(out_ref.shape[0]):
        out_ref[block] = mat[block * count : (block + 1) * count]


def one_kernel(gathered_ref, ready_ref, inv_ref, ship_ref, held_ref, blank_ref):
    blank(blank_ref)
    half, rows = gathered_ref.shape[2] // 2, held_ref.shape[1]
    ready = jnp.concatenate([ready_ref[block] for block in range(ready_ref.shape[0])], axis=0)
    for panel, mats in enumerate((woven(*masked(inv_ref, 0)), split(ready))):
        applied = apply_mat(gathered_ref, slice(panel * half, (panel + 1) * half), *mats)
        ship_ref[panel], held_ref[panel] = applied[:rows], applied[rows:]


def spread_kernel(mine_ref, other_ref, product_ref, own_ref, spread_ref, kept_ref):
    del product_ref, kept_ref
    own = jnp.where(lax.axis_index("prow") % 2 == 1, mine_ref[...], other_ref[...])
    own_ref[...] = own
    spread(spread_ref, own[1])


def columns_kernel(couple_ref, after_ref, spread_ref):
    del after_ref
    width = spread_ref.shape[2]
    lanes = pl.ds(pl.multiple_of(lax.axis_index("prow") // 2 * width, width), width)
    both = jnp.concatenate([couple_ref[0, :, lanes], couple_ref[1, :, lanes]], axis=0)
    spread(spread_ref, both)


def product_kernel(inv_ref, columns_ref, spread_ref, ship_ref, held_ref):
    blank(ship_ref)
    blank(held_ref)
    left = jnp.concatenate(masked(inv_ref, 0), axis=0)
    count, rows = columns_ref.shape[0], left.shape[0] // 2
    right = jnp.concatenate(
        [
            jnp.concatenate([columns_ref[block, part * rows : (part + 1) * rows] for block in range(count)], axis=0)
            for part in range(2)
        ],
        axis=1,
    )
    left_high, left_low = split(left)
    right_high, right_low = split(right)
    both = jnp.dot(jnp.concatenate([left_high, left_low], axis=0), right_high, preferred_element_type=F32)
    product = both[: 2 * rows] + both[2 * rows :] + jnp.dot(left_high, right_low, preferred_element_type=F32)
    half = product.shape[1] // 2
    for target in range(spread_ref.shape[0]):
        spread_ref[target, 0] = product[:rows, :half] + product[rows:, half:]
        spread_ref[target, 1] = product[rows:, :half] - product[:rows, half:]


def product_mats(product_ref):
    levels = product_ref.shape[0] // 2
    real = jnp.concatenate([product_ref[2 * level] for level in range(levels)], axis=1)
    imag = jnp.concatenate([product_ref[2 * level + 1] for level in range(levels)], axis=1)
    return woven(real, imag)


def weave_kernel(product_ref, mat_ref):
    depth = mat_ref.shape[0] // 2
    mat_ref[:depth, :], mat_ref[depth:, :] = product_mats(product_ref)


def zero_kernel(gathered_ref, mat_ref, other_ref, own_ref, out_ref):
    upper = lax.axis_index("prow") % 2 == 1
    depth, width = mat_ref.shape[0] // 2, out_ref.shape[3]

    def finish(mat_high, mat_low):
        zero = own_ref[0] - apply_mat(gathered_ref, slice(None), mat_high, mat_low)
        for panel, solved in enumerate((zero, own_ref[1])):
            for part in range(2):
                out_ref[part, :, panel, :] = solved[:, part * width : (part + 1) * width]

    @pl.when(upper)
    def _():
        finish(*product_mats(other_ref))

    @pl.when(jnp.logical_not(upper))
    def _():
        finish(mat_ref[:depth, :], mat_ref[depth:, :])


def call(kernel, out_shape, *args, aliases={}):
    return pl.pallas_call(
        kernel,
        in_specs=[VMEM] * len(args),
        out_specs=jax.tree.map(lambda array: VMEM, out_shape),
        out_shape=out_shape,
        input_output_aliases=aliases,
        compiler_params=pltpu.CompilerParams(vmem_limit_bytes=VMEM_LIMIT),
    )(*args)


def per_device(x_done, l_below, rhs_window, inv_diag, l_couple):
    columns, levels = lax.axis_size("pcol"), lax.axis_size("prow") // 2
    rows, width = 2 * rhs_window.shape[1], l_below.shape[2]
    block = inv_diag.shape[3] // levels
    upper = lax.axis_index("prow") % 2 == 1
    swap = [(device, device ^ 1) for device in range(2 * levels)]
    same_core = [[2 * level + core for level in range(levels)] for core in range(2)]
    array = lambda *shape: jax.ShapeDtypeStruct(shape, F32)
    over_columns = lambda value: lax.all_to_all(value, "pcol", 0, 0)
    over_levels = lambda value: lax.all_to_all(value, "prow", 0, 0, axis_index_groups=same_core)

    total = update(x_done, l_below, rows)
    total = call(subtract_kernel, array(*total.shape), rhs_window, total, aliases={1: 0})
    received = lax.ppermute(total, "prow", swap)
    parts = array(columns, 2 * width, block)

    share = lambda l_couple, inv_diag, after: over_columns(call(columns_kernel, parts, l_couple, after))
    ready = lambda l_couple, inv_diag, after: call(ready_kernel, parts, inv_diag, after)
    gathered = lax.cond(upper, ready, share, l_couple, inv_diag, total)
    summed = call(add_kernel, array(*total.shape), total, received, aliases={0: 0})
    own = array(2, rows // 2, 2 * width)
    whole = array(columns, rows, 2 * width)

    def solve(summed, inv_diag, ready):
        reduced = call(reduce_kernel, array(columns, rows, 4 * width), over_levels(summed))
        return tuple(call(one_kernel, [own, own, whole], over_columns(reduced), ready, inv_diag))

    def multiply(summed, inv_diag, gathered):
        del summed
        product = array(levels, 2, width, block)
        product, ship, held = call(product_kernel, [product, own, own], inv_diag, gathered)
        return ship, held, over_levels(product).reshape(whole.shape)

    ship, held, product = lax.cond(upper, solve, multiply, summed, inv_diag, gathered)
    shipped = lax.ppermute(ship, "prow", swap)
    mat = jax.ShapeDtypeStruct((4 * columns * width, 2 * width), BF)
    mat = call(weave_kernel, mat, product)
    one = array(columns, rows // 2, 2 * width)
    held, one, product = call(spread_kernel, [own, one, whole], held, shipped, product, aliases={2: 2})
    other = lax.ppermute(product, "prow", swap)
    return call(zero_kernel, array(*rhs_window.shape), over_columns(one), mat, other, held)


def solution(mesh):
    placed = (
        P(None, None, "prow"),
        P(None, None, "pcol", "prow"),
        P(None, "prow", None, "pcol"),
        P(None, None, "pcol", None),
        P(None, "pcol", None),
    )
    return jax.shard_map(
        per_device,
        mesh=mesh,
        in_specs=placed,
        out_specs=P(None, "prow", None, "pcol"),
        check_vma=False,
    )
```

```python
import functools

import jax
import jax.numpy as jnp
from jax import lax
from jax.experimental import pallas as pl
from jax.experimental.pallas import tpu as pltpu
from jax.sharding import PartitionSpec as P

BF = jnp.bfloat16
F32 = jnp.float32
PLAN = ((2, 256), (3, 512))
VMEM_LIMIT = 16 * 1024 * 1024
UPDATE_VMEM = 53 * 1024 * 1024
VMEM = pl.BlockSpec(memory_space=pltpu.VMEM)


def split(mat):
    high = mat.astype(BF)
    return high, (mat - high.astype(F32)).astype(BF)


def dot_split(left, right):
    left_high, left_low = split(left)
    right_high, right_low = split(right)
    return lax.dot_general(
        jnp.concatenate([left_high, left_low, left_high], axis=1),
        jnp.concatenate([right_high, right_high, right_low], axis=1),
        (((1,), (1,)), ((), ())),
        preferred_element_type=F32,
    )


def update_kernel(x_hbm, l_hbm, total, *scratch):
    groups = len(PLAN)
    x_bufs, l_bufs, sems = scratch[:groups], scratch[groups : 2 * groups], scratch[2 * groups]

    def copies(group, step):
        count, width = PLAN[group]
        first = sum(other for other, _ in PLAN[:group])
        start = sum(other * wide for other, wide in PLAN[:group])
        lanes = pl.ds(pl.multiple_of(start + step * width, 128), width)
        return (
            pltpu.make_async_copy(l_hbm.at[:, :, :, lanes], l_bufs[group].at[step], sems.at[first + step, 0]),
            pltpu.make_async_copy(x_hbm.at[:, :, lanes], x_bufs[group].at[step], sems.at[first + step, 1]),
        )

    def begin(group, step, carry):
        for copy in copies(group, step):
            copy.start()
        return carry

    def multiply(group, step, carry):
        for copy in copies(group, step):
            copy.wait()
        x_buf, l_buf = x_bufs[group], l_bufs[group]
        left = jnp.concatenate([x_buf[step, 0], x_buf[step, 1]], axis=1)
        rows = []
        for panel in range(2):
            real, imag = l_buf[step, 0, panel], l_buf[step, 1, panel]
            rows.append(jnp.concatenate([real, imag], axis=1))
            rows.append(jnp.concatenate([-imag, real], axis=1))
        total[...] += dot_split(left, jnp.concatenate(rows, axis=0))
        return carry

    for group in range(groups):
        lax.fori_loop(0, PLAN[group][0], functools.partial(begin, group), 0)
    total[...] = jnp.zeros_like(total)
    for group in range(groups):
        lax.fori_loop(0, PLAN[group][0], functools.partial(multiply, group), 0)


def update(x_done, l_below, rows):
    _, sides, depth = x_done.shape
    width = l_below.shape[2]
    return pl.pallas_call(
        update_kernel,
        in_specs=[pl.BlockSpec(memory_space=pltpu.HBM)] * 2,
        out_specs=VMEM,
        out_shape=jax.ShapeDtypeStruct((sides, 4 * width), F32),
        scratch_shapes=[
            *(pltpu.VMEM((count, 2, sides, chunk), F32) for count, chunk in PLAN),
            *(pltpu.VMEM((count, 2, 2, width, chunk), F32) for count, chunk in PLAN),
            pltpu.SemaphoreType.DMA((sum(count for count, _ in PLAN), 2)),
        ],
        compiler_params=pltpu.CompilerParams(vmem_limit_bytes=UPDATE_VMEM),
        cost_estimate=pl.CostEstimate(
            flops=2 * 3 * sides * 2 * depth * 4 * width, bytes_accessed=x_done.size * 4 + l_below.size * 4, transcendentals=0
        ),
    )(x_done, l_below).reshape(sides // rows, rows, 4 * width)


def subtract_kernel(rhs_ref, total_ref, out_ref):
    del total_ref
    rows = rhs_ref.shape[1]
    rhs = jnp.concatenate([rhs_ref[part, :, panel, :] for panel in range(2) for part in range(2)], axis=1)
    device = lax.axis_index("prow")
    own = pl.ds(pl.multiple_of(device % 2 * rows, rows), rows)
    out_ref[device // 2, own, :] -= rhs


def add_kernel(mine_ref, other_ref, out_ref):
    del mine_ref
    out_ref[...] += other_ref[...]


def reduce_kernel(parts_ref, spread_ref):
    total = parts_ref[0]
    for block in range(1, parts_ref.shape[0]):
        total = total + parts_ref[block]
    spread(spread_ref, -total)


def low_lanes(rows):
    return lax.broadcasted_iota(jnp.int32, (rows, 128), 1) < 64


def by_part(gathered_ref, lanes):
    low = low_lanes(gathered_ref.shape[1])
    real, imag = [], []
    for pair in range(gathered_ref.shape[0] // 2):
        first, second = gathered_ref[2 * pair, :, lanes], gathered_ref[2 * pair + 1, :, lanes]
        real.append(jnp.where(low, first, pltpu.roll(second, 64, 1)))
        imag.append(jnp.where(low, pltpu.roll(first, 64, 1), second))
    return jnp.concatenate([jnp.concatenate(real, axis=1), jnp.concatenate(imag, axis=1)], axis=0)


def apply_mat(gathered_ref, lanes, mat_high, mat_low):
    high, low = split(by_part(gathered_ref, lanes))
    rows = high.shape[0]
    both = jnp.dot(jnp.concatenate([high, low], axis=0), mat_high, preferred_element_type=F32)
    terms = both[:rows] + both[rows:] + jnp.dot(high, mat_low, preferred_element_type=F32)
    turned = pltpu.roll(terms[rows // 2 :], 64, 1)
    return terms[: rows // 2] + jnp.where(low_lanes(rows // 2), -turned, turned)


def masked(inv_ref, panel):
    shape = inv_ref.shape[2:]
    row_ids = lax.broadcasted_iota(jnp.int32, shape, 0) + lax.axis_index("pcol") * shape[0]
    upper = lax.broadcasted_iota(jnp.int32, shape, 1) >= row_ids
    return jnp.where(upper, inv_ref[0, panel], 0.0), jnp.where(upper, inv_ref[1, panel], 0.0)


def spread(out_ref, value):
    for target in range(out_ref.shape[0]):
        out_ref[target] = value


def blank(out_ref):
    out_ref[0] = jnp.zeros(out_ref.shape[1:], F32)


def turned_mat(real, imag):
    return jnp.concatenate([real, imag], axis=0).T


def ready_kernel(inv_ref, after_ref, out_ref):
    del after_ref
    blocks, count = out_ref.shape[0] // 2, out_ref.shape[1]
    for panel in range(2):
        mat = turned_mat(*masked(inv_ref, panel))
        for block in range(blocks):
            out_ref[panel * blocks + block] = mat[block * count : (block + 1) * count]


def one_kernel(gathered_ref, ready_ref, ship_ref, held_ref, blank_ref):
    blank(blank_ref)
    half, rows, blocks = gathered_ref.shape[2] // 2, held_ref.shape[1], ready_ref.shape[0] // 2
    for panel in range(2):
        mat = jnp.concatenate([ready_ref[panel * blocks + block] for block in range(blocks)], axis=0)
        applied = apply_mat(gathered_ref, slice(panel * half, (panel + 1) * half), *split(mat))
        ship_ref[panel], held_ref[panel] = applied[:rows], applied[rows:]


def spread_kernel(mine_ref, other_ref, product_ref, own_ref, spread_ref, kept_ref):
    del product_ref, kept_ref
    own = jnp.where(lax.axis_index("prow") % 2 == 1, mine_ref[...], other_ref[...])
    own_ref[...] = own
    spread(spread_ref, own[1])


def columns_kernel(couple_ref, after_ref, spread_ref):
    del after_ref
    width = spread_ref.shape[2]
    lanes = pl.ds(pl.multiple_of(lax.axis_index("prow") // 2 * width, width), width)
    both = jnp.concatenate([couple_ref[0, :, lanes], couple_ref[1, :, lanes]], axis=0)
    spread(spread_ref, both)


def product_kernel(inv_ref, columns_ref, spread_ref, ship_ref, held_ref):
    blank(ship_ref)
    blank(held_ref)
    left = jnp.concatenate(masked(inv_ref, 0), axis=0)
    count, rows = columns_ref.shape[0], left.shape[0] // 2
    right = jnp.concatenate(
        [
            jnp.concatenate([columns_ref[block, part * rows : (part + 1) * rows] for block in range(count)], axis=0)
            for part in range(2)
        ],
        axis=1,
    )
    left_high, left_low = split(left)
    right_high, right_low = split(right)
    both = jnp.dot(jnp.concatenate([left_high, left_low], axis=0), right_high, preferred_element_type=F32)
    product = both[: 2 * rows] + both[2 * rows :] + jnp.dot(left_high, right_low, preferred_element_type=F32)
    half = product.shape[1] // 2
    for target in range(spread_ref.shape[0]):
        spread_ref[target, 0] = product[:rows, :half] + product[rows:, half:]
        spread_ref[target, 1] = product[rows:, :half] - product[:rows, half:]


def product_mats(product_ref):
    levels = product_ref.shape[0] // 2
    real = jnp.concatenate([product_ref[2 * level] for level in range(levels)], axis=1)
    imag = jnp.concatenate([product_ref[2 * level + 1] for level in range(levels)], axis=1)
    return split(turned_mat(real, imag))


def turn_kernel(product_ref, mat_ref):
    depth = mat_ref.shape[0] // 2
    mat_ref[:depth, :], mat_ref[depth:, :] = product_mats(product_ref)


def zero_kernel(gathered_ref, mat_ref, other_ref, own_ref, out_ref):
    upper = lax.axis_index("prow") % 2 == 1
    depth, width = mat_ref.shape[0] // 2, out_ref.shape[3]

    def finish(mat_high, mat_low):
        zero = own_ref[0] - apply_mat(gathered_ref, slice(None), mat_high, mat_low)
        for panel, solved in enumerate((zero, own_ref[1])):
            for part in range(2):
                out_ref[part, :, panel, :] = solved[:, part * width : (part + 1) * width]

    @pl.when(upper)
    def _():
        finish(*product_mats(other_ref))

    @pl.when(jnp.logical_not(upper))
    def _():
        finish(mat_ref[:depth, :], mat_ref[depth:, :])


def call(kernel, out_shape, *args, aliases={}):
    return pl.pallas_call(
        kernel,
        in_specs=[VMEM] * len(args),
        out_specs=jax.tree.map(lambda array: VMEM, out_shape),
        out_shape=out_shape,
        input_output_aliases=aliases,
        compiler_params=pltpu.CompilerParams(vmem_limit_bytes=VMEM_LIMIT),
    )(*args)


def per_device(x_done, l_below, rhs_window, inv_diag, l_couple):
    columns, levels = lax.axis_size("pcol"), lax.axis_size("prow") // 2
    rows, width = 2 * rhs_window.shape[1], l_below.shape[2]
    block = inv_diag.shape[3] // levels
    upper = lax.axis_index("prow") % 2 == 1
    swap = [(device, device ^ 1) for device in range(2 * levels)]
    same_core = [[2 * level + core for level in range(levels)] for core in range(2)]
    array = lambda *shape: jax.ShapeDtypeStruct(shape, F32)
    over_columns = lambda value: lax.all_to_all(value, "pcol", 0, 0)
    over_levels = lambda value: lax.all_to_all(value, "prow", 0, 0, axis_index_groups=same_core)

    total = update(x_done, l_below, rows)
    total = call(subtract_kernel, array(*total.shape), rhs_window, total, aliases={1: 0})
    received = lax.ppermute(total, "prow", swap)
    parts = array(columns, 2 * width, block)

    share = lambda l_couple, inv_diag, after: over_columns(call(columns_kernel, parts, l_couple, after))
    ready = lambda l_couple, inv_diag, after: call(ready_kernel, parts, inv_diag, after)
    gathered = lax.cond(upper, ready, share, l_couple, inv_diag, total)
    summed = call(add_kernel, array(*total.shape), total, received, aliases={0: 0})
    own = array(2, rows // 2, 2 * width)
    whole = array(columns, rows, 2 * width)

    def solve(summed, inv_diag, ready):
        del inv_diag
        reduced = call(reduce_kernel, array(columns, rows, 4 * width), over_levels(summed))
        return tuple(call(one_kernel, [own, own, whole], over_columns(reduced), ready))

    def multiply(summed, inv_diag, gathered):
        del summed
        product = array(levels, 2, width, block)
        product, ship, held = call(product_kernel, [product, own, own], inv_diag, gathered)
        return ship, held, over_levels(product).reshape(whole.shape)

    ship, held, product = lax.cond(upper, solve, multiply, summed, inv_diag, gathered)
    shipped = lax.ppermute(ship, "prow", swap)
    mat = jax.ShapeDtypeStruct((2 * columns * width, 2 * width), BF)
    mat = call(turn_kernel, mat, product)
    one = array(columns, rows // 2, 2 * width)
    held, one, product = call(spread_kernel, [own, one, whole], held, shipped, product, aliases={2: 2})
    other = lax.ppermute(product, "prow", swap)
    return call(zero_kernel, array(*rhs_window.shape), over_columns(one), mat, other, held)


def solution(mesh):
    placed = (
        P(None, None, "prow"),
        P(None, None, "pcol", "prow"),
        P(None, "prow", None, "pcol"),
        P(None, None, "pcol", None),
        P(None, "pcol", None),
    )
    return jax.shard_map(
        per_device,
        mesh=mesh,
        in_specs=placed,
        out_specs=P(None, "prow", None, "pcol"),
        check_vma=False,
    )
```

```python
import functools

import jax
import jax.numpy as jnp
from jax import lax
from jax.experimental import pallas as pl
from jax.experimental.pallas import tpu as pltpu
from jax.sharding import PartitionSpec as P

BF = jnp.bfloat16
F32 = jnp.float32
PLAN = ((2, 256), (3, 512))
VMEM_LIMIT = 16 * 1024 * 1024
UPDATE_VMEM = 53 * 1024 * 1024
VMEM = pl.BlockSpec(memory_space=pltpu.VMEM)


def split(mat):
    high = mat.astype(BF)
    return high, (mat - high.astype(F32)).astype(BF)


def dot_split(left, right):
    left_high, left_low = split(left)
    right_high, right_low = split(right)
    return lax.dot_general(
        jnp.concatenate([left_high, left_low, left_high], axis=1),
        jnp.concatenate([right_high, right_high, right_low], axis=1),
        (((1,), (1,)), ((), ())),
        preferred_element_type=F32,
    )


def update_kernel(x_hbm, l_hbm, total, *scratch):
    groups = len(PLAN)
    x_bufs, l_bufs, sems = scratch[:groups], scratch[groups : 2 * groups], scratch[2 * groups]

    def copies(group, step):
        count, width = PLAN[group]
        first = sum(other for other, _ in PLAN[:group])
        start = sum(other * wide for other, wide in PLAN[:group])
        lanes = pl.ds(pl.multiple_of(start + step * width, 128), width)
        return (
            pltpu.make_async_copy(l_hbm.at[:, :, :, lanes], l_bufs[group].at[step], sems.at[first + step, 0]),
            pltpu.make_async_copy(x_hbm.at[:, :, lanes], x_bufs[group].at[step], sems.at[first + step, 1]),
        )

    def begin(group, step, carry):
        for copy in copies(group, step):
            copy.start()
        return carry

    def multiply(group, step, carry):
        for copy in copies(group, step):
            copy.wait()
        x_buf, l_buf = x_bufs[group], l_bufs[group]
        left = jnp.concatenate([x_buf[step, 0], x_buf[step, 1]], axis=1)
        rows = []
        for panel in range(2):
            real, imag = l_buf[step, 0, panel], l_buf[step, 1, panel]
            rows.append(jnp.concatenate([real, imag], axis=1))
            rows.append(jnp.concatenate([-imag, real], axis=1))
        total[...] += dot_split(left, jnp.concatenate(rows, axis=0))
        return carry

    for group in range(groups):
        lax.fori_loop(0, PLAN[group][0], functools.partial(begin, group), 0)
    total[...] = jnp.zeros_like(total)
    for group in range(groups):
        lax.fori_loop(0, PLAN[group][0], functools.partial(multiply, group), 0)


def update(x_done, l_below, rows):
    _, sides, depth = x_done.shape
    width = l_below.shape[2]
    return pl.pallas_call(
        update_kernel,
        in_specs=[pl.BlockSpec(memory_space=pltpu.HBM)] * 2,
        out_specs=VMEM,
        out_shape=jax.ShapeDtypeStruct((sides, 4 * width), F32),
        scratch_shapes=[
            *(pltpu.VMEM((count, 2, sides, chunk), F32) for count, chunk in PLAN),
            *(pltpu.VMEM((count, 2, 2, width, chunk), F32) for count, chunk in PLAN),
            pltpu.SemaphoreType.DMA((sum(count for count, _ in PLAN), 2)),
        ],
        compiler_params=pltpu.CompilerParams(vmem_limit_bytes=UPDATE_VMEM),
        cost_estimate=pl.CostEstimate(
            flops=2 * 3 * sides * 2 * depth * 4 * width, bytes_accessed=x_done.size * 4 + l_below.size * 4, transcendentals=0
        ),
    )(x_done, l_below).reshape(sides // rows, rows, 4 * width)


def subtract_kernel(rhs_ref, total_ref, out_ref):
    del total_ref
    rows = rhs_ref.shape[1]
    rhs = jnp.concatenate([rhs_ref[part, :, panel, :] for panel in range(2) for part in range(2)], axis=1)
    device = lax.axis_index("prow")
    own = pl.ds(pl.multiple_of(device % 2 * rows, rows), rows)
    out_ref[device // 2, own, :] -= rhs


def add_kernel(mine_ref, other_ref, out_ref):
    del mine_ref
    out_ref[...] += other_ref[...]


def reduce_kernel(parts_ref, spread_ref):
    total = parts_ref[0]
    for block in range(1, parts_ref.shape[0]):
        total = total + parts_ref[block]
    spread(spread_ref, -total)


def low_lanes(rows):
    return lax.broadcasted_iota(jnp.int32, (rows, 128), 1) < 64


def by_part(gathered_ref, lanes):
    low = low_lanes(gathered_ref.shape[1])
    real, imag = [], []
    for pair in range(gathered_ref.shape[0] // 2):
        first, second = gathered_ref[2 * pair, :, lanes], gathered_ref[2 * pair + 1, :, lanes]
        real.append(jnp.where(low, first, pltpu.roll(second, 64, 1)))
        imag.append(jnp.where(low, pltpu.roll(first, 64, 1), second))
    return jnp.concatenate([jnp.concatenate(real, axis=1), jnp.concatenate(imag, axis=1)], axis=0)


def apply_mat(gathered_ref, lanes, mat_high, mat_low):
    high, low = split(by_part(gathered_ref, lanes))
    rows = high.shape[0]
    both = jnp.dot(jnp.concatenate([high, low], axis=0), mat_high, preferred_element_type=F32)
    terms = both[:rows] + both[rows:] + jnp.dot(high, mat_low, preferred_element_type=F32)
    turned = pltpu.roll(terms[rows // 2 :], 64, 1)
    return terms[: rows // 2] + jnp.where(low_lanes(rows // 2), -turned, turned)


def masked(inv_ref, panel):
    shape = inv_ref.shape[2:]
    row_ids = lax.broadcasted_iota(jnp.int32, shape, 0) + lax.axis_index("pcol") * shape[0]
    upper = lax.broadcasted_iota(jnp.int32, shape, 1) >= row_ids
    return jnp.where(upper, inv_ref[0, panel], 0.0), jnp.where(upper, inv_ref[1, panel], 0.0)


def spread(out_ref, value):
    for target in range(out_ref.shape[0]):
        out_ref[target] = value


def blank(out_ref):
    out_ref[0] = jnp.zeros(out_ref.shape[1:], F32)


def turned_mat(real, imag):
    return jnp.concatenate([real, imag], axis=0).T


def ready_kernel(inv_ref, after_ref, out_ref):
    del after_ref
    blocks, count = out_ref.shape[0] // 2, out_ref.shape[1]
    for panel in range(2):
        mat = turned_mat(*masked(inv_ref, panel))
        for block in range(blocks):
            out_ref[panel * blocks + block] = mat[block * count : (block + 1) * count]


def one_kernel(gathered_ref, ready_ref, ship_ref, held_ref, blank_ref):
    blank(blank_ref)
    half, rows, blocks = gathered_ref.shape[2] // 2, held_ref.shape[1], ready_ref.shape[0] // 2
    for panel in range(2):
        mat = jnp.concatenate([ready_ref[panel * blocks + block] for block in range(blocks)], axis=0)
        applied = apply_mat(gathered_ref, slice(panel * half, (panel + 1) * half), *split(mat))
        ship_ref[panel], held_ref[panel] = applied[:rows], applied[rows:]


def spread_kernel(mine_ref, other_ref, product_ref, own_ref, spread_ref, kept_ref):
    del product_ref, kept_ref
    own = jnp.where(lax.axis_index("prow") % 2 == 1, mine_ref[...], other_ref[...])
    own_ref[...] = own
    spread(spread_ref, own[1])


def columns_kernel(couple_ref, after_ref, spread_ref):
    del after_ref
    width = spread_ref.shape[2]
    lanes = pl.ds(pl.multiple_of(lax.axis_index("prow") // 2 * width, width), width)
    both = jnp.concatenate([couple_ref[0, :, lanes], couple_ref[1, :, lanes]], axis=0)
    spread(spread_ref, both)


def product_kernel(inv_ref, columns_ref, spread_ref, ship_ref, held_ref):
    blank(ship_ref)
    blank(held_ref)
    left = jnp.concatenate(masked(inv_ref, 0), axis=0)
    count, rows = columns_ref.shape[0], left.shape[0] // 2
    right = jnp.concatenate(
        [
            jnp.concatenate([columns_ref[block, part * rows : (part + 1) * rows] for block in range(count)], axis=0)
            for part in range(2)
        ],
        axis=1,
    )
    left_high, left_low = split(left)
    right_high, right_low = split(right)
    both = jnp.dot(jnp.concatenate([left_high, left_low], axis=0), right_high, preferred_element_type=F32)
    product = both[: 2 * rows] + both[2 * rows :] + jnp.dot(left_high, right_low, preferred_element_type=F32)
    half = product.shape[1] // 2
    real = product[:rows, :half] + product[rows:, half:]
    imag = product[rows:, :half] - product[:rows, half:]
    for target in range(spread_ref.shape[0]):
        spread_ref[target, 0], spread_ref[target, 1] = real, imag


def product_mats(product_ref):
    levels = product_ref.shape[0] // 2
    real = jnp.concatenate([product_ref[2 * level] for level in range(levels)], axis=1)
    imag = jnp.concatenate([product_ref[2 * level + 1] for level in range(levels)], axis=1)
    return split(turned_mat(real, imag))


def turn_kernel(product_ref, mat_ref):
    depth = mat_ref.shape[0] // 2
    mat_ref[:depth, :], mat_ref[depth:, :] = product_mats(product_ref)


def zero_kernel(gathered_ref, mat_ref, other_ref, own_ref, out_ref):
    upper = lax.axis_index("prow") % 2 == 1
    depth, width = mat_ref.shape[0] // 2, out_ref.shape[3]

    def finish(mat_high, mat_low):
        zero = own_ref[0] - apply_mat(gathered_ref, slice(None), mat_high, mat_low)
        for panel, solved in enumerate((zero, own_ref[1])):
            for part in range(2):
                out_ref[part, :, panel, :] = solved[:, part * width : (part + 1) * width]

    @pl.when(upper)
    def _():
        finish(*product_mats(other_ref))

    @pl.when(jnp.logical_not(upper))
    def _():
        finish(mat_ref[:depth, :], mat_ref[depth:, :])


def call(kernel, out_shape, *args, aliases={}):
    return pl.pallas_call(
        kernel,
        in_specs=[VMEM] * len(args),
        out_specs=jax.tree.map(lambda array: VMEM, out_shape),
        out_shape=out_shape,
        input_output_aliases=aliases,
        compiler_params=pltpu.CompilerParams(vmem_limit_bytes=VMEM_LIMIT),
    )(*args)


def per_device(x_done, l_below, rhs_window, inv_diag, l_couple):
    columns, levels = lax.axis_size("pcol"), lax.axis_size("prow") // 2
    rows, width = 2 * rhs_window.shape[1], l_below.shape[2]
    block = inv_diag.shape[3] // levels
    upper = lax.axis_index("prow") % 2 == 1
    swap = [(device, device ^ 1) for device in range(2 * levels)]
    same_core = [[2 * level + core for level in range(levels)] for core in range(2)]
    array = lambda *shape: jax.ShapeDtypeStruct(shape, F32)
    over_columns = lambda value: lax.all_to_all(value, "pcol", 0, 0)
    over_levels = lambda value: lax.all_to_all(value, "prow", 0, 0, axis_index_groups=same_core)

    total = update(x_done, l_below, rows)
    total = call(subtract_kernel, array(*total.shape), rhs_window, total, aliases={1: 0})
    received = lax.ppermute(total, "prow", swap)
    parts = array(columns, 2 * width, block)

    share = lambda l_couple, inv_diag, after: over_columns(call(columns_kernel, parts, l_couple, after))
    ready = lambda l_couple, inv_diag, after: call(ready_kernel, parts, inv_diag, after)
    gathered = lax.cond(upper, ready, share, l_couple, inv_diag, total)
    summed = call(add_kernel, array(*total.shape), total, received, aliases={0: 0})
    own = array(2, rows // 2, 2 * width)
    whole = array(columns, rows, 2 * width)

    def solve(summed, inv_diag, ready):
        del inv_diag
        reduced = call(reduce_kernel, array(columns, rows, 4 * width), over_levels(summed))
        return tuple(call(one_kernel, [own, own, whole], over_columns(reduced), ready))

    def multiply(summed, inv_diag, gathered):
        del summed
        product = array(levels, 2, width, block)
        product, ship, held = call(product_kernel, [product, own, own], inv_diag, gathered)
        return ship, held, over_levels(product).reshape(whole.shape)

    ship, held, product = lax.cond(upper, solve, multiply, summed, inv_diag, gathered)
    shipped = lax.ppermute(ship, "prow", swap)
    mat = jax.ShapeDtypeStruct((2 * columns * width, 2 * width), BF)
    mat = call(turn_kernel, mat, product)
    one = array(columns, rows // 2, 2 * width)
    held, one, product = call(spread_kernel, [own, one, whole], held, shipped, product, aliases={2: 2})
    other = lax.ppermute(product, "prow", swap)
    return call(zero_kernel, array(*rhs_window.shape), over_columns(one), mat, other, held)


def solution(mesh):
    placed = (
        P(None, None, "prow"),
        P(None, None, "pcol", "prow"),
        P(None, "prow", None, "pcol"),
        P(None, None, "pcol", None),
        P(None, "pcol", None),
    )
    return jax.shard_map(
        per_device,
        mesh=mesh,
        in_specs=placed,
        out_specs=P(None, "prow", None, "pcol"),
        check_vma=False,
    )
```
